1024 devices in a mesh: grp: 16 (over x, core), rep: 64 (over z, y).
Axes of the slice: x: 8, y: 8, z: 8, core: 2. Of those that a mesh axis runs over, the one named last changes fastest.
Arguments:
- features: bfloat16 [524288, 768], P(('grp', 'rep')), may hold values from -6 to 6
- fetch_row: int32 [256, 4096], P('grp', 'rep'), may hold values from 0 to 511
- live_count: int32 [256, 64], P('grp', 'rep'), may hold values from 16 to 64, as said below
- seed_features: bfloat16 [524288, 768], P(('grp', 'rep')), may hold values from -6 to 6
- tile_block: int32 [4096, 8], P(('grp', 'rep')), may hold values from 0 to 7, each once within a row
- tile_weight: bfloat16 [4096, 8, 128, 128], P(('grp', 'rep')), may hold values from -0.1875 to 0.1875
- self_weight: bfloat16 [768, 512], replicated, may hold values from -0.21875 to 0.21875
- neighbour_weight: bfloat16 [768, 512], replicated, may hold values from -0.21875 to 0.21875
- layer_bias: float32 [512], replicated, may hold values from -4 to 4
- cotangent: bfloat16 [524288, 512], P(('grp', 'rep')), may hold values from -24 to 24
Outputs:
- weight_grad: float32 [512, 768], P('grp', 'rep')
The draws below stay inside these ranges and needn't reach their ends.
Inputs may be any that keep to these rules, and one draw needn't show every extreme that they name: `live_count`: slots at or past the count are padding. In every draw, for each rep index some owner is asked for all 64 slots by every device of its group. `tile_block`: each row names every block of a device's fetched rows once.
All inputs are finite; a program needn't handle non-finite values.
Results may differ from the reference program's by a relative error of at most 0.0043.
Values may be sent and summed in bfloat16 or wider, within the bound.
No kernel may reach another device: no remote copies, remote signals or barrier semaphores. Data moves between devices by JAX's collectives and lax.ppermute only.
A program may use at most 32 MiB of HBM per device.

```python
import jax
import jax.numpy as jnp
from jax import lax

FEAT = 768
HID = 512
TGT = 512
SLOTS = 64
ROWS_DEV = 512
FETCH = 1024
SEEDS = 524288
N_GRP = 16
N_REP = 64


def draw_live_count(key, part):
    key = jax.random.fold_in(key, 11)
    key_base, key_hot = jax.random.split(key)
    base_count = jax.random.randint(key_base, (N_GRP * N_GRP, N_REP), SLOTS // 4, SLOTS + 1)
    hot_owner = jax.random.randint(key_hot, (1, N_REP), 0, N_GRP)
    peer_ix = (jnp.arange(N_GRP * N_GRP, dtype=jnp.int32) % N_GRP)[:, None]
    return jnp.where(peer_ix == hot_owner, SLOTS, base_count).astype(jnp.int32)


def place_ends(values, key, least, largest):
    longest = values.shape.index(max(values.shape))
    spots = []
    for shift in (0, 1):
        where = [jax.random.randint(jax.random.fold_in(key, axis), (), 0, length) for axis, length in enumerate(values.shape)]
        where[longest] = (where[longest] + shift) % values.shape[longest]
        spots.append(tuple(where))
    return values.at[spots[0]].set(least).at[spots[1]].set(largest)


def with_spikes(entries, own_key, source, target, shards_of, factor):
    owner, partner = [(jnp.arange(entries.shape[position]) // (entries.shape[position] // shards_of)).reshape([-1 if axis == position else 1 for axis in range(entries.ndim)]) for position in (source, target)]
    chosen = jax.random.permutation(own_key, shards_of)[partner]
    strong = (owner == chosen) | (owner == (partner + shards_of // 2) % shards_of)
    return jnp.where(strong, factor * entries, entries)


def shard_levels(stream_key, dims, cuts, least, high):
    gain = 1.0
    for dim, blocks in cuts:
        heights = jax.random.uniform(jax.random.fold_in(jax.random.fold_in(stream_key, 6), dim), (blocks,), jnp.float32, least / len(cuts), high / len(cuts))
        gain = gain * jnp.repeat(jnp.exp(heights), dims[dim] // blocks).reshape((-1,) + (1,) * (len(dims) - 1 - dim))
    return gain


def noise(stream_key, shape, deviation, bound, shards=(), kind=jnp.bfloat16):
    array = jax.random.normal(stream_key, shape, jnp.float32) * deviation
    if len(shards) > 0:
        array = shard_levels(stream_key, shape, shards, -0.22, 0.18) * array
    return jnp.clip(array, min=-bound, max=bound).astype(kind)


def gaussian_with(own_key, shape, scale, limit, pieces, heavy, held_as=jnp.bfloat16):
    values = scale * jax.random.normal(own_key, shape, jnp.float32)
    if pieces:
        values = values * shard_levels(own_key, shape, pieces, -0.22, 0.18)
    return jnp.clip(with_spikes(values, jax.random.fold_in(own_key, 3), *heavy), -limit, limit).astype(held_as)


def setup_inputs(seed: int = 0) -> dict:
    key_of = jax.random.split(jax.random.key(seed), 11)
    features = noise(key_of[0], (N_GRP * N_REP * ROWS_DEV, FEAT), 1.0, 6.0, ((0, 1024),))
    fetch_row = place_ends(jax.random.randint(key_of[1], (N_GRP * N_GRP, N_REP * SLOTS), 0, ROWS_DEV), jax.random.fold_in(key_of[1], 1), 0, ROWS_DEV - 1).astype(jnp.int32)
    live_count = draw_live_count(jax.random.fold_in(key_of[10], 71), 0)
    seed_features = noise(key_of[3], (SEEDS, FEAT), 1.0, 6.0, ((0, 1024),))
    tile_block = jax.vmap(lambda own: jax.random.permutation(own, FETCH // 128))(jax.random.split(key_of[4], (SEEDS // 128))).reshape((SEEDS // 128, FETCH // 128)).astype(jnp.int32)
    tile_weight = noise(key_of[5], (SEEDS // 128, FETCH // 128, 128, 128), FETCH ** -0.5, 0.1875, ((0, 1024),))
    self_weight = noise(key_of[6], (FEAT, HID), FEAT ** -0.5, 0.21875)
    neighbour_weight = noise(key_of[7], (FEAT, HID), FEAT ** -0.5, 0.21875)
    layer_bias = noise(key_of[8], (HID,), 1.0, 4.0, (), jnp.float32)
    cotangent = gaussian_with(key_of[9], (SEEDS, HID), 1.0, 24.0, ((0, 1024),), (0, 1, 512, 6.0))
    return {"features": features, "fetch_row": fetch_row, "live_count": live_count, "seed_features": seed_features, "tile_block": tile_block, "tile_weight": tile_weight, "self_weight": self_weight, "neighbour_weight": neighbour_weight, "layer_bias": layer_bias, "cotangent": cotangent}


def reference(features, fetch_row, live_count, seed_features, tile_block, tile_weight, self_weight, neighbour_weight, layer_bias, cotangent):
    devices = N_GRP * N_REP
    fetch_blocks = N_GRP * SLOTS // 128
    seed_blocks = TGT // 128
    tables = features.reshape(N_GRP, N_REP, ROWS_DEV, FEAT)
    asked_all = fetch_row.reshape(N_GRP, N_GRP, N_REP, SLOTS)
    counts_all = live_count.reshape(N_GRP, N_GRP, N_REP)
    seeds_all = seed_features.reshape(devices, TGT, FEAT)
    block_all = tile_block.reshape(devices, seed_blocks, fetch_blocks)
    edges_all = tile_weight.reshape(devices, seed_blocks, fetch_blocks, 128, 128)
    cot_all = cotangent.reshape(devices, TGT, HID)
    peer_ix = jnp.arange(N_GRP, dtype=jnp.int32)
    slot_ix = jnp.arange(SLOTS, dtype=jnp.int32)
    self_f = self_weight.astype(jnp.float32)
    neigh_f = neighbour_weight.astype(jnp.float32)

    def accumulate(device, total):
        group_ix = device // N_REP
        rep_ix = device % N_REP
        asked = asked_all[group_ix, :, rep_ix, :]
        owner_tables = tables[:, rep_ix]
        table_rows = owner_tables[peer_ix[:, None], asked]
        live_mask = slot_ix[None, :] < counts_all[group_ix, :, rep_ix][:, None]
        table_rows = jnp.where(live_mask[:, :, None], table_rows, jnp.zeros((), jnp.bfloat16))
        row_blocks = table_rows.reshape(fetch_blocks, 128, FEAT)
        chosen = row_blocks[block_all[device]]
        aggregated = jnp.einsum("bkij,bkjf->bif", edges_all[device].astype(jnp.float32), chosen.astype(jnp.float32))
        aggregated = aggregated.reshape(TGT, FEAT).astype(jnp.bfloat16)
        seeds = seeds_all[device]
        pre_act = jnp.dot(seeds.astype(jnp.float32), self_f, preferred_element_type=jnp.float32)
        pre_act = pre_act + jnp.dot(aggregated.astype(jnp.float32), neigh_f, preferred_element_type=jnp.float32)
        pre_act = pre_act + layer_bias.astype(jnp.float32)[None, :]
        sigmoid_val = jax.nn.sigmoid(pre_act)
        slope = sigmoid_val * (1.0 + pre_act * (1.0 - sigmoid_val))
        grad_pre = (cot_all[device].astype(jnp.float32) * slope).astype(jnp.bfloat16)
        term = lax.dot_general(grad_pre.astype(jnp.float32), aggregated.astype(jnp.float32), (((0,), (0,)), ((), ())), preferred_element_type=jnp.float32)
        return total + term

    start_total = jnp.zeros((HID, FEAT), jnp.float32)
    return lax.fori_loop(0, devices, accumulate, start_total)
```

```python
import functools

import jax
import jax.numpy as jnp
from jax import lax
from jax.experimental import pallas as pl
from jax.experimental.pallas import tpu as pltpu
from jax.sharding import Mesh, PartitionSpec as P

F32 = jnp.float32
BF16 = jnp.bfloat16
GRP = ("x", "c")
REP = ("z", "y")
EVERY = GRP + REP
VMEM_LIMIT = 24 * 1024 * 1024


def whole(shape):
    return pl.BlockSpec(shape, lambda *_: (0,) * len(shape))


def params(grid_dims=0):
    semantics = ("arbitrary",) * grid_dims if grid_dims else None
    return pltpu.CompilerParams(vmem_limit_bytes=VMEM_LIMIT, dimension_semantics=semantics)


def pick_kernel(asked_ref, table_ref, out_ref, hot_ref):
    owners, slots = asked_ref.shape[0], asked_ref.shape[2]
    rows = table_ref.shape[0]
    line = lax.broadcasted_iota(jnp.int32, (slots, slots), 0)
    lane = lax.broadcasted_iota(jnp.int32, (slots, slots), 1)
    row_ix = lax.broadcasted_iota(jnp.int32, (slots, rows), 1).astype(F32)
    for p in range(owners):
        asked = jnp.broadcast_to(asked_ref[p].astype(F32), (slots, slots))
        column = jnp.sum(jnp.where(line == lane, asked, 0.0), axis=1, keepdims=True)
        hot_ref[p * slots : (p + 1) * slots, :] = jnp.where(row_ix == column, 1.0, 0.0).astype(BF16)
    out_ref[...] = jnp.dot(hot_ref[...], table_ref[...], preferred_element_type=F32).astype(BF16)


def pick_rows(asked, table):
    owners, _, slots = asked.shape
    rows, width = table.shape
    step = owners // 4
    return pl.pallas_call(
        pick_kernel,
        grid=(4,),
        out_shape=jax.ShapeDtypeStruct((owners * slots, width), BF16),
        in_specs=[pl.BlockSpec((step, 1, slots), lambda i: (i, 0, 0)), whole((rows, width))],
        out_specs=pl.BlockSpec((step * slots, width), lambda i: (i, 0)),
        scratch_shapes=[pltpu.VMEM((step * slots, rows), BF16)],
        compiler_params=params(1),
        cost_estimate=pl.CostEstimate(
            flops=2 * owners * slots * rows * width, bytes_accessed=5 * 10**6, transcendentals=0
        ),
        name="pick_rows",
    )(asked, table)


def prepare_kernel(block_ref, live_ref, weight_ref, seed_ref, self_ref, bias_ref, _, adj_ref, own_ref):
    seed_blocks, tiles, side, _ = weight_ref.shape
    slots = adj_ref.shape[1] // live_ref.shape[0]
    lane = lax.broadcasted_iota(jnp.int32, (side, side), 1)
    for b in range(seed_blocks):
        for k in range(tiles):
            block = block_ref[b, k]
            limit = jnp.where(lane < slots, live_ref[2 * block, 0], live_ref[2 * block + 1, 0] + slots)
            tile = jnp.where(lane < limit, weight_ref[b, k].astype(F32), 0.0)
            start = pl.multiple_of(block * side, side)
            adj_ref[b * side : (b + 1) * side, pl.ds(start, side)] = tile.astype(BF16)
    own_ref[...] = (
        jnp.dot(seed_ref[...], self_ref[...], preferred_element_type=F32) + bias_ref[...]
    )


def prepare(tile_block, live_count, tile_weight, seeds, self_weight, bias, after):
    seed_blocks, tiles, side, _ = tile_weight.shape
    targets, width = seeds.shape
    hidden = self_weight.shape[1]
    return pl.pallas_call(
        prepare_kernel,
        out_shape=(
            jax.ShapeDtypeStruct((seed_blocks * side, tiles * side), BF16),
            jax.ShapeDtypeStruct((targets, hidden), F32),
        ),
        in_specs=[
            pl.BlockSpec(memory_space=pltpu.SMEM),
            pl.BlockSpec(memory_space=pltpu.SMEM),
            pl.BlockSpec(memory_space=pltpu.VMEM),
            pl.BlockSpec(memory_space=pltpu.VMEM),
            pl.BlockSpec(memory_space=pltpu.VMEM),
            pl.BlockSpec(memory_space=pltpu.VMEM),
            pl.BlockSpec(memory_space=pl.ANY),
        ],
        out_specs=(pl.BlockSpec(memory_space=pltpu.VMEM), pl.BlockSpec(memory_space=pltpu.VMEM)),
        compiler_params=params(),
        cost_estimate=pl.CostEstimate(
            flops=2 * targets * width * hidden, bytes_accessed=6 * 10**6, transcendentals=0
        ),
        name="prepare",
    )(tile_block, live_count, tile_weight, seeds, self_weight, bias.reshape(1, -1), after)


def layer_kernel(core_ref, adj_ref, rows_ref, neigh_ref, own_ref, cot_ref, keep_ref, send_ref, agg_ref, pre_ref, grad_ref, out_ref):
    step, last = pl.program_id(0), pl.num_programs(0) - 1
    chunk = rows_ref.shape[1]
    agg = jnp.dot(adj_ref[...], rows_ref[...], preferred_element_type=F32).astype(BF16)
    agg_ref[:, pl.ds(pl.multiple_of(step * chunk, chunk), chunk)] = agg
    part = jnp.dot(agg, neigh_ref[...], preferred_element_type=F32)

    @pl.when(step == 0)
    def _():
        pre_ref[...] = own_ref[...] + part

    @pl.when((step > 0) & (step < last))
    def _():
        pre_ref[...] = pre_ref[...] + part

    @pl.when(step == last)
    def _():
        pre = pre_ref[...] + part
        s = 1.0 / (1.0 + jnp.exp(-pre))
        slope = s * (1.0 + pre * (1.0 - s))
        grad_ref[...] = (cot_ref[...].astype(F32) * slope).astype(BF16)
        out_ref[...] = lax.dot_general(
            grad_ref[...], agg_ref[...], (((0,), (0,)), ((), ())), preferred_element_type=F32
        )
        core = core_ref[0]
        groups, span = keep_ref.shape[0], keep_ref.shape[1]
        for x in range(groups):
            mine = pl.multiple_of((2 * x + core) * span, span)
            other = pl.multiple_of((2 * x + 1 - core) * span, span)
            keep_ref[x] = out_ref[pl.ds(mine, span), :]
            send_ref[x] = out_ref[pl.ds(other, span), :].astype(BF16)


def layer(core, adj, rows, neigh, own, cot, span):
    targets, fetched = adj.shape
    width, hidden = neigh.shape
    chunk = 256
    shape = (hidden // (2 * span), span, width)
    return pl.pallas_call(
        layer_kernel,
        grid=(width // chunk,),
        out_shape=(jax.ShapeDtypeStruct(shape, F32), jax.ShapeDtypeStruct(shape, BF16)),
        in_specs=[
            pl.BlockSpec(memory_space=pltpu.SMEM),
            whole((targets, fetched)),
            pl.BlockSpec((fetched, chunk), lambda i: (0, i)),
            pl.BlockSpec((chunk, hidden), lambda i: (i, 0)),
            whole((targets, hidden)),
            whole((targets, hidden)),
        ],
        out_specs=(whole(shape), whole(shape)),
        scratch_shapes=[
            pltpu.VMEM((targets, width), BF16),
            pltpu.VMEM((targets, hidden), F32),
            pltpu.VMEM((targets, hidden), BF16),
            pltpu.VMEM((hidden, width), F32),
        ],
        compiler_params=params(1),
        cost_estimate=pl.CostEstimate(
            flops=2 * targets * width * (fetched + 2 * hidden),
            bytes_accessed=8 * 10**6,
            transcendentals=targets * hidden,
        ),
        name="layer",
    )(core, adj, rows, neigh, own, cot)


def body(
    features,
    fetch_row,
    live_count,
    seed_features,
    tile_block,
    tile_weight,
    self_weight,
    neighbour_weight,
    layer_bias,
    cotangent,
):
    owners, slots = fetch_row.shape
    width, hidden = neighbour_weight.shape
    nx, nc, nz, ny = (lax.axis_size(a) for a in EVERY)
    span = hidden // (nx * nc)
    asked = lax.all_to_all(fetch_row.reshape(owners, 1, slots), GRP, split_axis=0, concat_axis=0, tiled=True)
    picked = pick_rows(asked, features)
    rows = lax.all_to_all(picked.reshape(owners, slots, width), GRP, split_axis=0, concat_axis=0, tiled=True)
    adj, own = prepare(tile_block, live_count, tile_weight, seed_features, self_weight, layer_bias, picked)
    core = lax.axis_index("c").astype(jnp.int32).reshape(1)
    keep, send = layer(core, adj, rows.reshape(owners * slots, width), neighbour_weight, own, cotangent, span)
    got = lax.ppermute(send, "c", [(0, 1), (1, 0)])
    pair = (keep + got.astype(F32)).astype(BF16)
    parts = lax.all_to_all(pair, "x", split_axis=0, concat_axis=0, tiled=True)
    ring = jnp.sum(parts.astype(F32), axis=0)
    cols = width // (nz * ny)
    pieces = ring.reshape(span, nz * ny, cols).transpose(1, 0, 2).reshape(nz * ny, span * cols)
    pieces = lax.all_to_all(pieces, REP, split_axis=0, concat_axis=0, tiled=True)
    return jnp.sum(pieces, axis=0).reshape(span, cols)


def solution(mesh):
    n_grp, n_rep = mesh.shape["grp"], mesh.shape["rep"]
    chips, lines = n_grp // 2, int(round(n_rep**0.5))
    fine = Mesh(mesh.devices.reshape(chips, 2, lines, n_rep // lines), EVERY)
    placed = (
        P(EVERY, None),
        P(GRP, REP),
        P(GRP, REP),
        P(EVERY, None),
        P(EVERY, None),
        P(EVERY, None, None, None),
        P(),
        P(),
        P(),
        P(EVERY, None),
    )
    return jax.shard_map(body, mesh=fine, in_specs=placed, out_specs=P(GRP, REP), check_vma=False)
```

```python
import jax
import jax.numpy as jnp
from jax import lax
from jax.experimental import pallas as pl
from jax.experimental.pallas import tpu as pltpu
from jax.sharding import Mesh, PartitionSpec as P

F32 = jnp.float32
BF16 = jnp.bfloat16
GRP = ("x", "c")
REP = ("z", "y")
EVERY = GRP + REP
VMEM_LIMIT = 24 * 1024 * 1024


def in_hbm(array):
    return pltpu.with_memory_space_constraint(array, pltpu.HBM)


def params():
    return pltpu.CompilerParams(vmem_limit_bytes=VMEM_LIMIT)


def pick_kernel(asked_ref, table_ref, out_ref, table_buf, hot_ref, out_buf, table_sem, out_sems):
    owners, slots = asked_ref.shape[0], asked_ref.shape[2]
    rows = table_ref.shape[0]
    load = pltpu.make_async_copy(table_ref, table_buf, table_sem)
    load.start()
    line = lax.broadcasted_iota(jnp.int32, (slots, slots), 0)
    lane = lax.broadcasted_iota(jnp.int32, (slots, slots), 1)
    row_ix = lax.broadcasted_iota(jnp.int32, (slots, rows), 1).astype(F32)
    for p in range(owners):
        asked = jnp.broadcast_to(asked_ref[p].astype(F32), (slots, slots))
        column = jnp.sum(jnp.where(line == lane, asked, 0.0), axis=1, keepdims=True)
        hot_ref[p * slots : (p + 1) * slots, :] = jnp.where(row_ix == column, 1.0, 0.0).astype(BF16)
    load.wait()
    pieces = out_sems.shape[0]
    size = owners * slots // pieces
    stores = []
    for i in range(pieces):
        part = pl.ds(i * size, size)
        out_buf[part, :] = jnp.dot(hot_ref[part, :], table_buf[...], preferred_element_type=F32).astype(BF16)
        stores.append(pltpu.make_async_copy(out_buf.at[part], out_ref.at[part], out_sems.at[i]))
        stores[i].start()
    for store in stores:
        store.wait()


def pick_rows(asked, table):
    owners, _, slots = asked.shape
    rows, width = table.shape
    pieces = 4
    return pl.pallas_call(
        pick_kernel,
        out_shape=pltpu.HBM((owners * slots, width), BF16),
        in_specs=[pl.BlockSpec(memory_space=pltpu.VMEM), pl.BlockSpec(memory_space=pltpu.HBM)],
        out_specs=pl.BlockSpec(memory_space=pltpu.HBM),
        scratch_shapes=[
            pltpu.VMEM((rows, width), BF16),
            pltpu.VMEM((owners * slots, rows), BF16),
            pltpu.VMEM((owners * slots, width), BF16),
            pltpu.SemaphoreType.DMA,
            pltpu.SemaphoreType.DMA((pieces,)),
        ],
        compiler_params=params(),
        cost_estimate=pl.CostEstimate(
            flops=2 * owners * slots * rows * width, bytes_accessed=5 * 10**6, transcendentals=0
        ),
        name="pick_rows",
    )(asked, in_hbm(table))


def prepare_kernel(block_ref, live_ref, weight_ref, seed_ref, self_ref, bias_ref, _, adj_ref, own_ref):
    seed_blocks, tiles, side, _ = weight_ref.shape
    slots = adj_ref.shape[1] // live_ref.shape[0]
    lane = lax.broadcasted_iota(jnp.int32, (side, side), 1)
    for b in range(seed_blocks):
        for k in range(tiles):
            block = block_ref[b, k]
            limit = jnp.where(lane < slots, live_ref[2 * block, 0], live_ref[2 * block + 1, 0] + slots)
            tile = jnp.where(lane < limit, weight_ref[b, k].astype(F32), 0.0)
            start = pl.multiple_of(block * side, side)
            adj_ref[b * side : (b + 1) * side, pl.ds(start, side)] = tile.astype(BF16)
    own_ref[...] = (
        jnp.dot(seed_ref[...], self_ref[...], preferred_element_type=F32) + bias_ref[...]
    )


def prepare(tile_block, live_count, tile_weight, seeds, self_weight, bias, after):
    seed_blocks, tiles, side, _ = tile_weight.shape
    targets, width = seeds.shape
    hidden = self_weight.shape[1]
    return pl.pallas_call(
        prepare_kernel,
        out_shape=(
            pltpu.HBM((seed_blocks * side, tiles * side), BF16),
            pltpu.HBM((targets, hidden), F32),
        ),
        in_specs=[
            pl.BlockSpec(memory_space=pltpu.SMEM),
            pl.BlockSpec(memory_space=pltpu.SMEM),
            pl.BlockSpec(memory_space=pltpu.VMEM),
            pl.BlockSpec(memory_space=pltpu.VMEM),
            pl.BlockSpec(memory_space=pltpu.VMEM),
            pl.BlockSpec(memory_space=pltpu.VMEM),
            pl.BlockSpec(memory_space=pl.ANY),
        ],
        out_specs=(pl.BlockSpec(memory_space=pltpu.VMEM), pl.BlockSpec(memory_space=pltpu.VMEM)),
        compiler_params=params(),
        cost_estimate=pl.CostEstimate(
            flops=2 * targets * width * hidden, bytes_accessed=6 * 10**6, transcendentals=0
        ),
        name="prepare",
    )(tile_block, live_count, tile_weight, seeds, self_weight, bias.reshape(1, -1), in_hbm(after))


def layer_kernel(
    core_ref, adj_hbm, rows_ref, neigh_hbm, own_hbm, cot_hbm, keep_ref, send_ref,
    adj_ref, neigh_ref, own_ref, cot_ref, agg_ref, out_ref, sems,
):
    pairs = [(adj_hbm, adj_ref), (neigh_hbm, neigh_ref), (own_hbm, own_ref), (cot_hbm, cot_ref)]
    loads = [pltpu.make_async_copy(src, dst, sems.at[i]) for i, (src, dst) in enumerate(pairs)]
    for load in loads:
        load.start()
    loads[0].wait()
    chunk = 256
    for start in range(0, rows_ref.shape[1], chunk):
        part = slice(start, start + chunk)
        agg = jnp.dot(adj_ref[...], rows_ref[:, part], preferred_element_type=F32)
        agg_ref[:, part] = agg.astype(BF16)
    for load in loads[1:]:
        load.wait()
    pre = own_ref[...] + jnp.dot(agg_ref[...], neigh_ref[...], preferred_element_type=F32)
    s = 1.0 / (1.0 + jnp.exp(-pre))
    slope = s * (1.0 + pre * (1.0 - s))
    grad = (cot_ref[...].astype(F32) * slope).astype(BF16)
    out_ref[...] = lax.dot_general(grad, agg_ref[...], (((0,), (0,)), ((), ())), preferred_element_type=F32)
    groups, span = keep_ref.shape[0], keep_ref.shape[1]

    def share(core):
        for x in range(groups):
            mine, other = (2 * x + core) * span, (2 * x + 1 - core) * span
            keep_ref[x] = out_ref[mine : mine + span, :]
            send_ref[x] = out_ref[other : other + span, :].astype(BF16)

    @pl.when(core_ref[0] == 0)
    def _():
        share(0)

    @pl.when(core_ref[0] == 1)
    def _():
        share(1)


def layer(core, adj, rows, neigh, own, cot, span):
    targets, fetched = adj.shape
    width, hidden = neigh.shape
    shape = (hidden // (2 * span), span, width)
    in_vmem, far = pl.BlockSpec(memory_space=pltpu.VMEM), pl.BlockSpec(memory_space=pltpu.HBM)
    return pl.pallas_call(
        layer_kernel,
        out_shape=(pltpu.VMEM(shape, F32), pltpu.VMEM(shape, BF16)),
        in_specs=[pl.BlockSpec(memory_space=pltpu.SMEM), far, in_vmem, far, far, far],
        out_specs=(in_vmem, in_vmem),
        scratch_shapes=[
            pltpu.VMEM((targets, fetched), BF16),
            pltpu.VMEM((width, hidden), BF16),
            pltpu.VMEM((targets, hidden), F32),
            pltpu.VMEM((targets, hidden), BF16),
            pltpu.VMEM((targets, width), BF16),
            pltpu.VMEM((hidden, width), F32),
            pltpu.SemaphoreType.DMA((4,)),
        ],
        compiler_params=params(),
        cost_estimate=pl.CostEstimate(
            flops=2 * targets * width * (fetched + 2 * hidden),
            bytes_accessed=8 * 10**6,
            transcendentals=targets * hidden,
        ),
        name="layer",
    )(core, in_hbm(adj), rows, in_hbm(neigh), in_hbm(own), in_hbm(cot))


def body(
    features,
    fetch_row,
    live_count,
    seed_features,
    tile_block,
    tile_weight,
    self_weight,
    neighbour_weight,
    layer_bias,
    cotangent,
):
    owners, slots = fetch_row.shape
    width, hidden = neighbour_weight.shape
    nx, nc, nz, ny = (lax.axis_size(a) for a in EVERY)
    span = hidden // (nx * nc)
    asked = lax.all_to_all(fetch_row.reshape(owners, 1, slots), GRP, split_axis=0, concat_axis=0, tiled=True)
    picked = pick_rows(asked, features)
    rows = lax.all_to_all(picked.reshape(owners, slots, width), GRP, split_axis=0, concat_axis=0, tiled=True)
    adj, own = prepare(tile_block, live_count, tile_weight, seed_features, self_weight, layer_bias, picked)
    core = lax.axis_index("c").astype(jnp.int32).reshape(1)
    keep, send = layer(core, adj, rows.reshape(owners * slots, width), neighbour_weight, own, cotangent, span)
    got = lax.ppermute(send, "c", [(0, 1), (1, 0)])
    pair = (keep + got.astype(F32)).astype(BF16)
    parts = lax.all_to_all(pair, "x", split_axis=0, concat_axis=0, tiled=True)
    ring = jnp.sum(parts.astype(F32), axis=0)
    cols = width // (nz * ny)
    pieces = ring.reshape(span, nz * ny, cols).transpose(1, 2, 0).reshape(nz * ny, cols * span)
    pieces = lax.all_to_all(pieces, REP, split_axis=0, concat_axis=0, tiled=True)
    return jnp.sum(pieces, axis=0).reshape(cols, span).T


def solution(mesh):
    n_grp, n_rep = mesh.shape["grp"], mesh.shape["rep"]
    chips, lines = n_grp // 2, int(round(n_rep**0.5))
    fine = Mesh(mesh.devices.reshape(chips, 2, lines, n_rep // lines), EVERY)
    placed = (
        P(EVERY, None),
        P(GRP, REP),
        P(GRP, REP),
        P(EVERY, None),
        P(EVERY, None),
        P(EVERY, None, None, None),
        P(),
        P(),
        P(),
        P(EVERY, None),
    )
    return jax.shard_map(body, mesh=fine, in_specs=placed, out_specs=P(GRP, REP), check_vma=False)
```

```python
import functools

import jax
import jax.numpy as jnp
from jax import lax
from jax.experimental import pallas as pl
from jax.experimental.pallas import tpu as pltpu
from jax.sharding import Mesh, PartitionSpec as P

F32 = jnp.float32
BF16 = jnp.bfloat16
GRP = ("x", "c")
REP = ("z", "y")
EVERY = GRP + REP
VMEM_LIMIT = 24 * 1024 * 1024


def in_hbm(array):
    return pltpu.with_memory_space_constraint(array, pltpu.HBM)


def params():
    return pltpu.CompilerParams(vmem_limit_bytes=VMEM_LIMIT)


def pick_kernel(asked_ref, table_ref, out_ref, table_buf, hot_ref, out_buf, table_sem, out_sems):
    owners, slots = asked_ref.shape[0], asked_ref.shape[2]
    rows = table_ref.shape[0]
    load = pltpu.make_async_copy(table_ref, table_buf, table_sem)
    load.start()
    line = lax.broadcasted_iota(jnp.int32, (slots, slots), 0)
    lane = lax.broadcasted_iota(jnp.int32, (slots, slots), 1)
    row_ix = lax.broadcasted_iota(jnp.int32, (slots, rows), 1).astype(F32)

    def build(first, last):
        for p in range(first, last):
            asked = jnp.broadcast_to(asked_ref[p].astype(F32), (slots, slots))
            column = jnp.sum(jnp.where(line == lane, asked, 0.0), axis=1, keepdims=True)
            hot_ref[p * slots : (p + 1) * slots, :] = jnp.where(row_ix == column, 1.0, 0.0).astype(BF16)

    pieces = out_sems.shape[0]
    each, early = owners // pieces, owners // 2
    size = each * slots
    build(0, early)
    load.wait()
    stores = []
    for i in range(pieces):
        build(max(i * each, early), max((i + 1) * each, early))
        part = pl.ds(i * size, size)
        out_buf[part, :] = jnp.dot(hot_ref[part, :], table_buf[...], preferred_element_type=F32).astype(BF16)
        stores.append(pltpu.make_async_copy(out_buf.at[part], out_ref.at[part], out_sems.at[i]))
        stores[i].start()
    for store in stores:
        store.wait()


def pick_rows(asked, table):
    owners, _, slots = asked.shape
    rows, width = table.shape
    pieces = 8
    return pl.pallas_call(
        pick_kernel,
        out_shape=pltpu.HBM((owners * slots, width), BF16),
        in_specs=[pl.BlockSpec(memory_space=pltpu.VMEM), pl.BlockSpec(memory_space=pltpu.HBM)],
        out_specs=pl.BlockSpec(memory_space=pltpu.HBM),
        scratch_shapes=[
            pltpu.VMEM((rows, width), BF16),
            pltpu.VMEM((owners * slots, rows), BF16),
            pltpu.VMEM((owners * slots, width), BF16),
            pltpu.SemaphoreType.DMA,
            pltpu.SemaphoreType.DMA((pieces,)),
        ],
        compiler_params=params(),
        cost_estimate=pl.CostEstimate(
            flops=2 * owners * slots * rows * width, bytes_accessed=5 * 10**6, transcendentals=0
        ),
        name="pick_rows",
    )(asked, in_hbm(table))


def core_major(array, span):
    starts = [(2 * x + core) * span for core in range(2) for x in range(array.shape[1] // (2 * span))]
    return jnp.concatenate([array[:, start : start + span] for start in starts], axis=1)


def prepare_kernel(
    span, block_ref, live_ref, weight_ref, seed_ref, self_ref, bias_ref, neigh_ref, cot_ref, _,
    adj_ref, own_ref, neigh_out, cot_out,
):
    seed_blocks, tiles, side, _ = weight_ref.shape
    slots = adj_ref.shape[1] // live_ref.shape[0]
    lane = lax.broadcasted_iota(jnp.int32, (side, side), 1)
    for b in range(seed_blocks):
        for k in range(tiles):
            block = block_ref[b, k]
            limit = jnp.where(lane < slots, live_ref[2 * block, 0], live_ref[2 * block + 1, 0] + slots)
            tile = jnp.where(lane < limit, weight_ref[b, k].astype(F32), 0.0)
            start = pl.multiple_of(block * side, side)
            adj_ref[b * side : (b + 1) * side, pl.ds(start, side)] = tile.astype(BF16)
    own = jnp.dot(seed_ref[...], self_ref[...], preferred_element_type=F32) + bias_ref[...]
    own_ref[...] = core_major(own, span)
    neigh_out[...] = core_major(neigh_ref[...], span)
    cot_out[...] = core_major(cot_ref[...], span)


def prepare(tile_block, live_count, tile_weight, seeds, self_weight, bias, neigh, cot, after, span):
    seed_blocks, tiles, side, _ = tile_weight.shape
    targets, width = seeds.shape
    hidden = self_weight.shape[1]
    near, far = pl.BlockSpec(memory_space=pltpu.VMEM), pl.BlockSpec(memory_space=pltpu.HBM)
    table = pl.BlockSpec(memory_space=pltpu.SMEM)
    return pl.pallas_call(
        functools.partial(prepare_kernel, span),
        out_shape=(
            pltpu.HBM((seed_blocks * side, tiles * side), BF16),
            pltpu.HBM((targets, hidden), F32),
            pltpu.HBM(neigh.shape, BF16),
            pltpu.HBM(cot.shape, BF16),
        ),
        in_specs=[table, table, near, near, near, near, near, near, far],
        out_specs=(near, near, near, near),
        compiler_params=params(),
        cost_estimate=pl.CostEstimate(
            flops=2 * targets * width * hidden, bytes_accessed=8 * 10**6, transcendentals=0
        ),
        name="prepare",
    )(tile_block, live_count, tile_weight, seeds, self_weight, bias.reshape(1, -1), neigh, cot, in_hbm(after))


def turned(left, right):
    return lax.dot_general(left, right, (((0,), (0,)), ((), ())), preferred_element_type=F32)


def layer_kernel(
    core_ref, adj_hbm, rows_ref, neigh_hbm, own_hbm, cot_hbm, send_ref, mine_ref, agg_ref,
    adj_ref, neigh_ref, own_ref, cot_ref, grad_ref, sems,
):
    pairs = [(adj_hbm, adj_ref), (neigh_hbm, neigh_ref), (own_hbm, own_ref), (cot_hbm, cot_ref)]
    loads = [pltpu.make_async_copy(src, dst, sems.at[i]) for i, (src, dst) in enumerate(pairs)]
    for load in loads:
        load.start()
    loads[0].wait()
    agg_ref[...] = jnp.dot(adj_ref[...], rows_ref[...], preferred_element_type=F32).astype(BF16)
    for load in loads[1:]:
        load.wait()
    targets, half = mine_ref.shape
    step = targets // 4
    for start in range(0, targets, step):
        part = slice(start, start + step)
        pre = own_ref[part, :] + jnp.dot(agg_ref[part, :], neigh_ref[...], preferred_element_type=F32)
        s = 1.0 / (1.0 + jnp.exp(-pre))
        slope = s * (1.0 + pre * (1.0 - s))
        grad_ref[part, :] = (cot_ref[part, :].astype(F32) * slope).astype(BF16)
    mine = pl.multiple_of(core_ref[0] * half, half)
    other = pl.multiple_of((1 - core_ref[0]) * half, half)
    mine_ref[...] = grad_ref[:, pl.ds(mine, half)]
    send_ref[...] = turned(grad_ref[:, pl.ds(other, half)], agg_ref[...]).astype(BF16)


def layer(core, adj, rows, neigh, own, cot):
    targets, fetched = adj.shape
    width, hidden = neigh.shape
    near, far = pl.BlockSpec(memory_space=pltpu.VMEM), pl.BlockSpec(memory_space=pltpu.HBM)
    return pl.pallas_call(
        layer_kernel,
        out_shape=(
            pltpu.VMEM((hidden // 2, width), BF16),
            pltpu.VMEM((targets, hidden // 2), BF16),
            pltpu.VMEM((targets, width), BF16),
        ),
        in_specs=[pl.BlockSpec(memory_space=pltpu.SMEM), far, near, far, far, far],
        out_specs=(near, near, near),
        scratch_shapes=[
            pltpu.VMEM((targets, fetched), BF16),
            pltpu.VMEM((width, hidden), BF16),
            pltpu.VMEM((targets, hidden), F32),
            pltpu.VMEM((targets, hidden), BF16),
            pltpu.VMEM((targets, hidden), BF16),
            pltpu.SemaphoreType.DMA((4,)),
        ],
        compiler_params=params(),
        cost_estimate=pl.CostEstimate(
            flops=2 * targets * width * (fetched + 2 * hidden),
            bytes_accessed=8 * 10**6,
            transcendentals=targets * hidden,
        ),
        name="layer",
    )(core, in_hbm(adj), rows, in_hbm(neigh), in_hbm(own), in_hbm(cot))


def own_term_kernel(mine_ref, agg_ref, keep_ref):
    keep_ref[...] = turned(mine_ref[...], agg_ref[...])


def own_term(mine, agg):
    targets, half = mine.shape
    width = agg.shape[1]
    near = pl.BlockSpec(memory_space=pltpu.VMEM)
    return pl.pallas_call(
        own_term_kernel,
        out_shape=pltpu.VMEM((half, width), F32),
        in_specs=[near, near],
        out_specs=near,
        compiler_params=params(),
        cost_estimate=pl.CostEstimate(
            flops=2 * targets * width * half, bytes_accessed=2 * 10**6, transcendentals=0
        ),
        name="own_term",
    )(mine, agg)


def body(
    features,
    fetch_row,
    live_count,
    seed_features,
    tile_block,
    tile_weight,
    self_weight,
    neighbour_weight,
    layer_bias,
    cotangent,
):
    owners, slots = fetch_row.shape
    width, hidden = neighbour_weight.shape
    nx, nc, nz, ny = (lax.axis_size(a) for a in EVERY)
    span = hidden // (nx * nc)
    asked = lax.all_to_all(fetch_row.reshape(owners, 1, slots), GRP, split_axis=0, concat_axis=0, tiled=True)
    picked = pick_rows(asked, features)
    rows = lax.all_to_all(picked.reshape(owners, slots, width), GRP, split_axis=0, concat_axis=0, tiled=True)
    adj, own, neigh, cot = prepare(
        tile_block, live_count, tile_weight, seed_features, self_weight, layer_bias, neighbour_weight, cotangent, picked, span
    )
    core = lax.axis_index("c").astype(jnp.int32).reshape(1)
    send, mine, agg = layer(core, adj, rows.reshape(owners * slots, width), neigh, own, cot)
    got = lax.ppermute(send, "c", [(0, 1), (1, 0)])
    keep = own_term(mine, agg)
    pair = (keep + got.astype(F32)).astype(BF16).reshape(nx, span, width)
    parts = lax.all_to_all(pair, "x", split_axis=0, concat_axis=0, tiled=True)
    ring = jnp.sum(parts.astype(F32), axis=0)
    cols = width // (nz * ny)
    pieces = ring.reshape(span, nz * ny, cols).transpose(1, 2, 0).reshape(nz * ny, cols * span)
    pieces = lax.all_to_all(pieces, REP, split_axis=0, concat_axis=0, tiled=True)
    return jnp.sum(pieces, axis=0).reshape(cols, span).T


def solution(mesh):
    n_grp, n_rep = mesh.shape["grp"], mesh.shape["rep"]
    chips, lines = n_grp // 2, int(round(n_rep**0.5))
    fine = Mesh(mesh.devices.reshape(chips, 2, lines, n_rep // lines), EVERY)
    placed = (
        P(EVERY, None),
        P(GRP, REP),
        P(GRP, REP),
        P(EVERY, None),
        P(EVERY, None),
        P(EVERY, None, None, None),
        P(),
        P(),
        P(),
        P(EVERY, None),
    )
    return jax.shard_map(body, mesh=fine, in_specs=placed, out_specs=P(GRP, REP), check_vma=False)
```

```python
import functools

import jax
import jax.numpy as jnp
from jax import lax
from jax.experimental import pallas as pl
from jax.experimental.pallas import tpu as pltpu
from jax.sharding import Mesh, PartitionSpec as P

F32 = jnp.float32
BF16 = jnp.bfloat16
GRP = ("x", "c")
REP = ("z", "y")
EVERY = GRP + REP
VMEM_LIMIT = 24 * 1024 * 1024


def in_vmem(array):
    return pltpu.with_memory_space_constraint(array, pltpu.VMEM)


def in_hbm(array):
    return pltpu.with_memory_space_constraint(array, pltpu.HBM)


def params():
    return pltpu.CompilerParams(vmem_limit_bytes=VMEM_LIMIT)


def pick_kernel(asked_ref, table_ref, out_ref, hot_ref, out_buf, out_sems):
    owners, slots = asked_ref.shape[0], asked_ref.shape[2]
    rows = table_ref.shape[0]
    line = lax.broadcasted_iota(jnp.int32, (slots, slots), 0)
    lane = lax.broadcasted_iota(jnp.int32, (slots, slots), 1)
    row_ix = lax.broadcasted_iota(jnp.int32, (slots, rows), 1).astype(F32)

    def build(first, last):
        for p in range(first, last):
            asked = jnp.broadcast_to(asked_ref[p].astype(F32), (slots, slots))
            column = jnp.sum(jnp.where(line == lane, asked, 0.0), axis=1, keepdims=True)
            hot_ref[p * slots : (p + 1) * slots, :] = jnp.where(row_ix == column, 1.0, 0.0).astype(BF16)

    pieces = out_sems.shape[0]
    each, early = owners // pieces, owners // 2
    size = each * slots
    build(0, early)
    stores = []
    for i in range(pieces):
        build(max(i * each, early), max((i + 1) * each, early))
        part = pl.ds(i * size, size)
        out_buf[part, :] = jnp.dot(hot_ref[part, :], table_ref[...], preferred_element_type=F32).astype(BF16)
        stores.append(pltpu.make_async_copy(out_buf.at[part], out_ref.at[part], out_sems.at[i]))
        stores[i].start()
    for store in stores:
        store.wait()


def stage_kernel(table_ref, out_ref, sem):
    load = pltpu.make_async_copy(table_ref, out_ref, sem)
    load.start()
    load.wait()


def stage(table):
    return pl.pallas_call(
        stage_kernel,
        out_shape=pltpu.VMEM(table.shape, table.dtype),
        in_specs=[pl.BlockSpec(memory_space=pltpu.HBM)],
        out_specs=pl.BlockSpec(memory_space=pltpu.VMEM),
        scratch_shapes=[pltpu.SemaphoreType.DMA],
        compiler_params=params(),
        cost_estimate=pl.CostEstimate(flops=0, bytes_accessed=2 * 10**6, transcendentals=0),
        name="stage",
    )(in_hbm(table))


def pick_rows(asked, table):
    owners, _, slots = asked.shape
    rows, width = table.shape
    pieces = 8
    return pl.pallas_call(
        pick_kernel,
        out_shape=pltpu.HBM((owners * slots, width), BF16),
        in_specs=[pl.BlockSpec(memory_space=pltpu.VMEM), pl.BlockSpec(memory_space=pltpu.VMEM)],
        out_specs=pl.BlockSpec(memory_space=pltpu.HBM),
        scratch_shapes=[
            pltpu.VMEM((owners * slots, rows), BF16),
            pltpu.VMEM((owners * slots, width), BF16),
            pltpu.SemaphoreType.DMA((pieces,)),
        ],
        compiler_params=params(),
        cost_estimate=pl.CostEstimate(
            flops=2 * owners * slots * rows * width, bytes_accessed=5 * 10**6, transcendentals=0
        ),
        name="pick_rows",
    )(asked, in_vmem(table))


def core_major(array, span):
    starts = [(2 * x + core) * span for core in range(2) for x in range(array.shape[1] // (2 * span))]
    return jnp.concatenate([array[:, start : start + span] for start in starts], axis=1)


def prepare_kernel(
    span, block_ref, live_ref, weight_ref, seed_ref, self_ref, bias_ref, neigh_ref, cot_ref, _,
    adj_ref, own_ref, neigh_out, cot_out,
):
    seed_blocks, tiles, side, _ = weight_ref.shape
    slots = adj_ref.shape[1] // live_ref.shape[0]
    lane = lax.broadcasted_iota(jnp.int32, (side, side), 1)
    for b in range(seed_blocks):
        for k in range(tiles):
            block = block_ref[b, k]
            limit = jnp.where(lane < slots, live_ref[2 * block, 0], live_ref[2 * block + 1, 0] + slots)
            tile = jnp.where(lane < limit, weight_ref[b, k].astype(F32), 0.0)
            start = pl.multiple_of(block * side, side)
            adj_ref[b * side : (b + 1) * side, pl.ds(start, side)] = tile.astype(BF16)
    own = jnp.dot(seed_ref[...], self_ref[...], preferred_element_type=F32) + bias_ref[...]
    own_ref[...] = core_major(own, span)
    neigh_out[...] = core_major(neigh_ref[...], span)
    cot_out[...] = core_major(cot_ref[...], span)


def prepare(tile_block, live_count, tile_weight, seeds, self_weight, bias, neigh, cot, after, span):
    seed_blocks, tiles, side, _ = tile_weight.shape
    targets, width = seeds.shape
    hidden = self_weight.shape[1]
    near, far = pl.BlockSpec(memory_space=pltpu.VMEM), pl.BlockSpec(memory_space=pltpu.HBM)
    table = pl.BlockSpec(memory_space=pltpu.SMEM)
    return pl.pallas_call(
        functools.partial(prepare_kernel, span),
        out_shape=(
            pltpu.HBM((seed_blocks * side, tiles * side), BF16),
            pltpu.HBM((targets, hidden), F32),
            pltpu.HBM(neigh.shape, BF16),
            pltpu.HBM(cot.shape, BF16),
        ),
        in_specs=[table, table, near, near, near, near, near, near, far],
        out_specs=(near, near, near, near),
        compiler_params=params(),
        cost_estimate=pl.CostEstimate(
            flops=2 * targets * width * hidden, bytes_accessed=8 * 10**6, transcendentals=0
        ),
        name="prepare",
    )(tile_block, live_count, tile_weight, seeds, self_weight, bias.reshape(1, -1), neigh, cot, in_hbm(after))


def turned(left, right):
    return lax.dot_general(left, right, (((0,), (0,)), ((), ())), preferred_element_type=F32)


def layer_kernel(
    core_ref, adj_hbm, rows_ref, neigh_hbm, own_hbm, cot_hbm, send_ref, mine_ref, agg_ref,
    adj_ref, neigh_ref, own_ref, cot_ref, grad_ref, sems,
):
    pairs = [(adj_hbm, adj_ref), (neigh_hbm, neigh_ref), (own_hbm, own_ref), (cot_hbm, cot_ref)]
    loads = [pltpu.make_async_copy(src, dst, sems.at[i]) for i, (src, dst) in enumerate(pairs)]
    for load in loads:
        load.start()
    loads[0].wait()
    agg_ref[...] = jnp.dot(adj_ref[...], rows_ref[...], preferred_element_type=F32).astype(BF16)
    for load in loads[1:]:
        load.wait()
    targets, half = mine_ref.shape
    step = targets // 4
    for start in range(0, targets, step):
        part = slice(start, start + step)
        pre = own_ref[part, :] + jnp.dot(agg_ref[part, :], neigh_ref[...], preferred_element_type=F32)
        s = 1.0 / (1.0 + jnp.exp(-pre))
        slope = s * (1.0 + pre * (1.0 - s))
        grad_ref[part, :] = (cot_ref[part, :].astype(F32) * slope).astype(BF16)
    mine = pl.multiple_of(core_ref[0] * half, half)
    other = pl.multiple_of((1 - core_ref[0]) * half, half)
    mine_ref[...] = grad_ref[:, pl.ds(mine, half)]
    send_ref[...] = turned(grad_ref[:, pl.ds(other, half)], agg_ref[...]).astype(BF16)


def layer(core, adj, rows, neigh, own, cot):
    targets, fetched = adj.shape
    width, hidden = neigh.shape
    near, far = pl.BlockSpec(memory_space=pltpu.VMEM), pl.BlockSpec(memory_space=pltpu.HBM)
    return pl.pallas_call(
        layer_kernel,
        out_shape=(
            pltpu.VMEM((hidden // 2, width), BF16),
            pltpu.VMEM((targets, hidden // 2), BF16),
            pltpu.VMEM((targets, width), BF16),
        ),
        in_specs=[pl.BlockSpec(memory_space=pltpu.SMEM), far, near, far, far, far],
        out_specs=(near, near, near),
        scratch_shapes=[
            pltpu.VMEM((targets, fetched), BF16),
            pltpu.VMEM((width, hidden), BF16),
            pltpu.VMEM((targets, hidden), F32),
            pltpu.VMEM((targets, hidden), BF16),
            pltpu.VMEM((targets, hidden), BF16),
            pltpu.SemaphoreType.DMA((4,)),
        ],
        compiler_params=params(),
        cost_estimate=pl.CostEstimate(
            flops=2 * targets * width * (fetched + 2 * hidden),
            bytes_accessed=8 * 10**6,
            transcendentals=targets * hidden,
        ),
        name="layer",
    )(core, in_hbm(adj), rows, in_hbm(neigh), in_hbm(own), in_hbm(cot))


def own_term_kernel(mine_ref, agg_ref, keep_ref):
    keep_ref[...] = turned(mine_ref[...], agg_ref[...])


def own_term(mine, agg):
    targets, half = mine.shape
    width = agg.shape[1]
    near = pl.BlockSpec(memory_space=pltpu.VMEM)
    return pl.pallas_call(
        own_term_kernel,
        out_shape=pltpu.VMEM((half, width), F32),
        in_specs=[near, near],
        out_specs=near,
        compiler_params=params(),
        cost_estimate=pl.CostEstimate(
            flops=2 * targets * width * half, bytes_accessed=2 * 10**6, transcendentals=0
        ),
        name="own_term",
    )(mine, agg)


def body(
    features,
    fetch_row,
    live_count,
    seed_features,
    tile_block,
    tile_weight,
    self_weight,
    neighbour_weight,
    layer_bias,
    cotangent,
):
    owners, slots = fetch_row.shape
    width, hidden = neighbour_weight.shape
    nx, nc, nz, ny = (lax.axis_size(a) for a in EVERY)
    span = hidden // (nx * nc)
    asked = lax.all_to_all(fetch_row.reshape(owners, 1, slots), GRP, split_axis=0, concat_axis=0, tiled=True)
    picked = pick_rows(asked, stage(features))
    rows = lax.all_to_all(picked.reshape(owners, slots, width), GRP, split_axis=0, concat_axis=0, tiled=True)
    adj, own, neigh, cot = prepare(
        tile_block, live_count, tile_weight, seed_features, self_weight, layer_bias, neighbour_weight, cotangent, picked, span
    )
    core = lax.axis_index("c").astype(jnp.int32).reshape(1)
    send, mine, agg = layer(core, adj, rows.reshape(owners * slots, width), neigh, own, cot)
    got = lax.ppermute(send, "c", [(0, 1), (1, 0)])
    keep = own_term(mine, agg)
    pair = (keep + got.astype(F32)).astype(BF16).reshape(nx, span, width)
    parts = lax.all_to_all(pair, "x", split_axis=0, concat_axis=0, tiled=True)
    ring = jnp.sum(parts.astype(F32), axis=0)
    cols = width // (nz * ny)
    pieces = ring.reshape(span, nz * ny, cols).transpose(1, 2, 0).reshape(nz * ny, cols * span)
    pieces = lax.all_to_all(pieces, REP, split_axis=0, concat_axis=0, tiled=True)
    return jnp.sum(pieces, axis=0).reshape(cols, span).T


def solution(mesh):
    n_grp, n_rep = mesh.shape["grp"], mesh.shape["rep"]
    chips, lines = n_grp // 2, int(round(n_rep**0.5))
    fine = Mesh(mesh.devices.reshape(chips, 2, lines, n_rep // lines), EVERY)
    placed = (
        P(EVERY, None),
        P(GRP, REP),
        P(GRP, REP),
        P(EVERY, None),
        P(EVERY, None),
        P(EVERY, None, None, None),
        P(),
        P(),
        P(),
        P(EVERY, None),
    )
    return jax.shard_map(body, mesh=fine, in_specs=placed, out_specs=P(GRP, REP), check_vma=False)
```

```python
import functools

import jax
import jax.numpy as jnp
from jax import lax
from jax.experimental import pallas as pl
from jax.experimental.pallas import tpu as pltpu
from jax.sharding import Mesh, PartitionSpec as P

F32 = jnp.float32
BF16 = jnp.bfloat16
GRP = ("x", "c")
REP = ("z", "y")
EVERY = GRP + REP
VMEM_LIMIT = 24 * 1024 * 1024


def in_vmem(array):
    return pltpu.with_memory_space_constraint(array, pltpu.VMEM)


def in_hbm(array):
    return pltpu.with_memory_space_constraint(array, pltpu.HBM)


def params():
    return pltpu.CompilerParams(vmem_limit_bytes=VMEM_LIMIT)


def pick_kernel(asked_ref, table_ref, out_ref, hot_ref, out_buf, out_sems):
    owners, slots = asked_ref.shape[0], asked_ref.shape[2]
    rows = table_ref.shape[0]
    line = lax.broadcasted_iota(jnp.int32, (slots, slots), 0)
    lane = lax.broadcasted_iota(jnp.int32, (slots, slots), 1)
    row_ix = lax.broadcasted_iota(jnp.int32, (slots, rows), 1).astype(F32)

    def build(first, last):
        for p in range(first, last):
            asked = jnp.broadcast_to(asked_ref[p].astype(F32), (slots, slots))
            column = jnp.sum(jnp.where(line == lane, asked, 0.0), axis=1, keepdims=True)
            hot_ref[p * slots : (p + 1) * slots, :] = jnp.where(row_ix == column, 1.0, 0.0).astype(BF16)

    pieces = out_sems.shape[0]
    each, early = owners // pieces, owners // 2
    size = each * slots
    build(0, early)
    stores = []
    for i in range(pieces):
        build(max(i * each, early), max((i + 1) * each, early))
        part = pl.ds(i * size, size)
        out_buf[part, :] = jnp.dot(hot_ref[part, :], table_ref[...], preferred_element_type=F32).astype(BF16)
        stores.append(pltpu.make_async_copy(out_buf.at[part], out_ref.at[part], out_sems.at[i]))
        stores[i].start()
    for store in stores:
        store.wait()


def stage_kernel(
    block_ref, live_ref, weight_hbm, table_hbm, seed_hbm, self_hbm, bias_ref, adj_hbm, own_hbm, table_ref,
    weight_ref, adj_ref, seed_ref, self_ref, own_ref, sems, out_sems,
):
    seed_blocks, tiles, side, _ = weight_ref.shape
    pairs = [(weight_hbm.at[b], weight_ref.at[b]) for b in range(seed_blocks)]
    pairs += [(seed_hbm, seed_ref), (self_hbm, self_ref), (table_hbm, table_ref)]
    loads = [pltpu.make_async_copy(src, dst, sems.at[i]) for i, (src, dst) in enumerate(pairs)]
    for load in loads:
        load.start()
    slots = adj_ref.shape[1] // live_ref.shape[1]
    lane = lax.broadcasted_iota(jnp.int32, (side, side), 1)
    stores = []
    for b in range(seed_blocks):
        loads[b].wait()
        lines = slice(b * side, (b + 1) * side)
        for k in range(tiles):
            block = block_ref[b, k]
            limit = jnp.where(lane < slots, live_ref[0, 2 * block], live_ref[0, 2 * block + 1] + slots)
            tile = jnp.where(lane < limit, weight_ref[b, k].astype(F32), 0.0)
            start = pl.multiple_of(block * side, side)
            adj_ref[lines, pl.ds(start, side)] = tile.astype(BF16)
        part = pl.ds(b * side, side)
        stores.append(pltpu.make_async_copy(adj_ref.at[part], adj_hbm.at[part], out_sems.at[b]))
        stores[b].start()
    for load in loads[seed_blocks:]:
        load.wait()
    for b in range(seed_blocks):
        part = pl.ds(b * side, side)
        own_ref[part, :] = jnp.dot(seed_ref[part, :], self_ref[...], preferred_element_type=F32) + bias_ref[...]
        stores.append(pltpu.make_async_copy(own_ref.at[part], own_hbm.at[part], out_sems.at[seed_blocks + b]))
        stores[seed_blocks + b].start()
    for store in stores:
        store.wait()


def stage(tile_block, live_count, tile_weight, table, seeds, self_weight, bias):
    seed_blocks, tiles, side, _ = tile_weight.shape
    targets, hidden = seeds.shape[0], self_weight.shape[1]
    near, far = pl.BlockSpec(memory_space=pltpu.VMEM), pl.BlockSpec(memory_space=pltpu.HBM)
    scalars = pl.BlockSpec(memory_space=pltpu.SMEM)
    shape = (seed_blocks * side, tiles * side)
    return pl.pallas_call(
        stage_kernel,
        out_shape=(pltpu.HBM(shape, BF16), pltpu.HBM((targets, hidden), F32), pltpu.VMEM(table.shape, BF16)),
        in_specs=[scalars, scalars, far, far, far, far, near],
        out_specs=(far, far, near),
        scratch_shapes=[
            pltpu.VMEM(tile_weight.shape, BF16),
            pltpu.VMEM(shape, BF16),
            pltpu.VMEM(seeds.shape, BF16),
            pltpu.VMEM(self_weight.shape, BF16),
            pltpu.VMEM((targets, hidden), F32),
            pltpu.SemaphoreType.DMA((seed_blocks + 3,)),
            pltpu.SemaphoreType.DMA((2 * seed_blocks,)),
        ],
        compiler_params=params(),
        cost_estimate=pl.CostEstimate(
            flops=2 * targets * seeds.shape[1] * hidden, bytes_accessed=7 * 10**6, transcendentals=0
        ),
        name="stage",
    )(
        in_hbm(tile_block),
        in_hbm(live_count.reshape(1, -1)),
        in_hbm(tile_weight),
        in_hbm(table),
        in_hbm(seeds),
        in_hbm(self_weight),
        in_hbm(bias.reshape(1, -1)),
    )


def pick_rows(asked, table):
    owners, _, slots = asked.shape
    rows, width = table.shape
    pieces = 8
    return pl.pallas_call(
        pick_kernel,
        out_shape=pltpu.HBM((owners * slots, width), BF16),
        in_specs=[pl.BlockSpec(memory_space=pltpu.VMEM), pl.BlockSpec(memory_space=pltpu.VMEM)],
        out_specs=pl.BlockSpec(memory_space=pltpu.HBM),
        scratch_shapes=[
            pltpu.VMEM((owners * slots, rows), BF16),
            pltpu.VMEM((owners * slots, width), BF16),
            pltpu.SemaphoreType.DMA((pieces,)),
        ],
        compiler_params=params(),
        cost_estimate=pl.CostEstimate(
            flops=2 * owners * slots * rows * width, bytes_accessed=5 * 10**6, transcendentals=0
        ),
        name="pick_rows",
    )(asked, in_vmem(table))


def turned(left, right):
    return lax.dot_general(left, right, (((0,), (0,)), ((), ())), preferred_element_type=F32)


def units_of(grad, core, span):
    hidden = grad.shape[1]
    unit = lax.broadcasted_iota(jnp.int32, (hidden, hidden // 2), 0)
    place = lax.broadcasted_iota(jnp.int32, (hidden, hidden // 2), 1)
    chosen = unit == place + (place // span + core) * span
    return jnp.dot(grad, jnp.where(chosen, 1.0, 0.0).astype(BF16), preferred_element_type=F32).astype(BF16)


def layer_kernel(
    span, core_ref, adj_ref, rows_ref, neigh_ref, own_hbm, cot_hbm, send_ref, grad_ref, agg_ref,
    own_ref, cot_ref, sems,
):
    pairs = [(own_hbm, own_ref), (cot_hbm, cot_ref)]
    loads = [pltpu.make_async_copy(src, dst, sems.at[i]) for i, (src, dst) in enumerate(pairs)]
    for load in loads:
        load.start()
    agg_ref[...] = jnp.dot(adj_ref[...], rows_ref[...], preferred_element_type=F32).astype(BF16)
    for load in loads:
        load.wait()
    targets = grad_ref.shape[0]
    step = targets // 4
    for start in range(0, targets, step):
        part = slice(start, start + step)
        pre = own_ref[part, :] + jnp.dot(agg_ref[part, :], neigh_ref[...], preferred_element_type=F32)
        s = 1.0 / (1.0 + jnp.exp(-pre))
        slope = s * (1.0 + pre * (1.0 - s))
        grad_ref[part, :] = (cot_ref[part, :].astype(F32) * slope).astype(BF16)
    other = units_of(grad_ref[...], 1 - core_ref[0], span)
    send_ref[...] = turned(other, agg_ref[...]).astype(BF16)


def layer(core, adj, rows, neigh, own, cot, span):
    targets, fetched = adj.shape
    width, hidden = neigh.shape
    near, far = pl.BlockSpec(memory_space=pltpu.VMEM), pl.BlockSpec(memory_space=pltpu.HBM)
    return pl.pallas_call(
        functools.partial(layer_kernel, span),
        out_shape=(
            pltpu.VMEM((hidden // 2, width), BF16),
            pltpu.VMEM((targets, hidden), BF16),
            pltpu.VMEM((targets, width), BF16),
        ),
        in_specs=[pl.BlockSpec(memory_space=pltpu.SMEM), near, near, near, far, far],
        out_specs=(near, near, near),
        scratch_shapes=[
            pltpu.VMEM((targets, hidden), F32),
            pltpu.VMEM((targets, hidden), BF16),
            pltpu.SemaphoreType.DMA((2,)),
        ],
        compiler_params=params(),
        cost_estimate=pl.CostEstimate(
            flops=2 * targets * width * (fetched + 2 * hidden),
            bytes_accessed=8 * 10**6,
            transcendentals=targets * hidden,
        ),
        name="layer",
    )(core, adj, rows, neigh, in_hbm(own), in_hbm(cot))


def own_term_kernel(span, core_ref, grad_ref, agg_ref, keep_ref):
    keep_ref[...] = turned(units_of(grad_ref[...], core_ref[0], span), agg_ref[...])


def own_term(core, grad, agg, span):
    targets, hidden = grad.shape
    width = agg.shape[1]
    near = pl.BlockSpec(memory_space=pltpu.VMEM)
    return pl.pallas_call(
        functools.partial(own_term_kernel, span),
        out_shape=pltpu.VMEM((hidden // 2, width), F32),
        in_specs=[pl.BlockSpec(memory_space=pltpu.SMEM), near, near],
        out_specs=near,
        compiler_params=params(),
        cost_estimate=pl.CostEstimate(
            flops=2 * targets * (width + hidden) * (hidden // 2), bytes_accessed=2 * 10**6, transcendentals=0
        ),
        name="own_term",
    )(core, grad, agg)


def body(
    features,
    fetch_row,
    live_count,
    seed_features,
    tile_block,
    tile_weight,
    self_weight,
    neighbour_weight,
    layer_bias,
    cotangent,
):
    owners, slots = fetch_row.shape
    width, hidden = neighbour_weight.shape
    nx, nc, nz, ny = (lax.axis_size(a) for a in EVERY)
    span = hidden // (nx * nc)
    asked = lax.all_to_all(fetch_row.reshape(owners, 1, slots), GRP, split_axis=0, concat_axis=0, tiled=True)
    adj, own, table = stage(
        tile_block, live_count, tile_weight, features, seed_features, self_weight, layer_bias
    )
    picked = pick_rows(asked, table)
    rows = lax.all_to_all(picked.reshape(owners, slots, width), GRP, split_axis=0, concat_axis=0, tiled=True)
    core = lax.axis_index("c").astype(jnp.int32).reshape(1)
    send, grad, agg = layer(
        core, adj, rows.reshape(owners * slots, width), neighbour_weight, own, cotangent, span
    )
    got = lax.ppermute(send, "c", [(0, 1), (1, 0)])
    keep = own_term(core, grad, agg, span)
    pair = (keep + got.astype(F32)).astype(BF16).reshape(nx, span, width)
    parts = lax.all_to_all(pair, "x", split_axis=0, concat_axis=0, tiled=True)
    ring = jnp.sum(parts.astype(F32), axis=0)
    cols = width // (nz * ny)
    pieces = ring.reshape(span, nz * ny, cols).transpose(1, 2, 0).reshape(nz * ny, cols * span)
    pieces = lax.all_to_all(pieces, REP, split_axis=0, concat_axis=0, tiled=True)
    return jnp.sum(pieces, axis=0).reshape(cols, span).T


def solution(mesh):
    n_grp, n_rep = mesh.shape["grp"], mesh.shape["rep"]
    chips, lines = n_grp // 2, int(round(n_rep**0.5))
    fine = Mesh(mesh.devices.reshape(chips, 2, lines, n_rep // lines), EVERY)
    placed = (
        P(EVERY, None),
        P(GRP, REP),
        P(GRP, REP),
        P(EVERY, None),
        P(EVERY, None),
        P(EVERY, None, None, None),
        P(),
        P(),
        P(),
        P(EVERY, None),
    )
    return jax.shard_map(body, mesh=fine, in_specs=placed, out_specs=P(GRP, REP), check_vma=False)
```

```python
import functools

import jax
import jax.numpy as jnp
import numpy as np
from jax import lax
from jax.experimental import pallas as pl
from jax.experimental.pallas import tpu as pltpu
from jax.sharding import Mesh, PartitionSpec as P

F32 = jnp.float32
BF16 = jnp.bfloat16
GRP = ("x", "c")
REP = ("z", "y")
EVERY = GRP + REP
VMEM_LIMIT = 24 * 1024 * 1024


def in_vmem(array):
    return pltpu.with_memory_space_constraint(array, pltpu.VMEM)


def in_hbm(array):
    return pltpu.with_memory_space_constraint(array, pltpu.HBM)


def params():
    return pltpu.CompilerParams(vmem_limit_bytes=VMEM_LIMIT)


def pick_kernel(asked_ref, table_ref, out_ref, hot_ref, out_buf, out_sems):
    owners, slots = asked_ref.shape[0], asked_ref.shape[2]
    rows = table_ref.shape[0]
    line = lax.broadcasted_iota(jnp.int32, (slots, slots), 0)
    lane = lax.broadcasted_iota(jnp.int32, (slots, slots), 1)
    row_ix = lax.broadcasted_iota(jnp.int32, (slots, rows), 1).astype(F32)

    def build(first, last):
        for p in range(first, last):
            asked = jnp.broadcast_to(asked_ref[p].astype(F32), (slots, slots))
            column = jnp.sum(jnp.where(line == lane, asked, 0.0), axis=1, keepdims=True)
            hot_ref[p * slots : (p + 1) * slots, :] = jnp.where(row_ix == column, 1.0, 0.0).astype(BF16)

    pieces = out_sems.shape[0]
    each, early = owners // pieces, owners // 2
    size = each * slots
    build(0, early)
    stores = []
    for i in range(pieces):
        build(max(i * each, early), max((i + 1) * each, early))
        part = pl.ds(i * size, size)
        out_buf[part, :] = jnp.dot(hot_ref[part, :], table_ref[...], preferred_element_type=F32).astype(BF16)
        stores.append(pltpu.make_async_copy(out_buf.at[part], out_ref.at[part], out_sems.at[i]))
        stores[i].start()
    for store in stores:
        store.wait()


def stage_kernel(
    block_ref, live_ref, weight_hbm, table_hbm, seed_hbm, self_hbm, bias_ref, adj_hbm, own_hbm, table_ref,
    weight_ref, adj_ref, seed_ref, self_ref, own_ref, sems, out_sems,
):
    seed_blocks, tiles, side, _ = weight_ref.shape
    pairs = [(weight_hbm.at[b], weight_ref.at[b]) for b in range(seed_blocks)]
    pairs += [(seed_hbm, seed_ref), (self_hbm, self_ref), (table_hbm, table_ref)]
    loads = [pltpu.make_async_copy(src, dst, sems.at[i]) for i, (src, dst) in enumerate(pairs)]
    for load in loads:
        load.start()
    slots = adj_ref.shape[1] // live_ref.shape[1]
    lane = lax.broadcasted_iota(jnp.int32, (side, side), 1)
    stores = []
    for b in range(seed_blocks):
        loads[b].wait()
        lines = slice(b * side, (b + 1) * side)
        for k in range(tiles):
            block = block_ref[b, k]
            limit = jnp.where(lane < slots, live_ref[0, 2 * block], live_ref[0, 2 * block + 1] + slots)
            tile = jnp.where(lane < limit, weight_ref[b, k].astype(F32), 0.0)
            start = pl.multiple_of(block * side, side)
            adj_ref[lines, pl.ds(start, side)] = tile.astype(BF16)
        part = pl.ds(b * side, side)
        stores.append(pltpu.make_async_copy(adj_ref.at[part], adj_hbm.at[part], out_sems.at[b]))
        stores[b].start()
    for load in loads[seed_blocks:]:
        load.wait()
    for b in range(seed_blocks):
        part = pl.ds(b * side, side)
        own_ref[part, :] = jnp.dot(seed_ref[part, :], self_ref[...], preferred_element_type=F32) + bias_ref[...]
        stores.append(pltpu.make_async_copy(own_ref.at[part], own_hbm.at[part], out_sems.at[seed_blocks + b]))
        stores[seed_blocks + b].start()
    for store in stores:
        store.wait()


def stage(tile_block, live_count, tile_weight, table, seeds, self_weight, bias):
    seed_blocks, tiles, side, _ = tile_weight.shape
    targets, hidden = seeds.shape[0], self_weight.shape[1]
    near, far = pl.BlockSpec(memory_space=pltpu.VMEM), pl.BlockSpec(memory_space=pltpu.HBM)
    scalars = pl.BlockSpec(memory_space=pltpu.SMEM)
    shape = (seed_blocks * side, tiles * side)
    return pl.pallas_call(
        stage_kernel,
        out_shape=(pltpu.HBM(shape, BF16), pltpu.HBM((targets, hidden), F32), pltpu.VMEM(table.shape, BF16)),
        in_specs=[scalars, scalars, far, far, far, far, near],
        out_specs=(far, far, near),
        scratch_shapes=[
            pltpu.VMEM(tile_weight.shape, BF16),
            pltpu.VMEM(shape, BF16),
            pltpu.VMEM(seeds.shape, BF16),
            pltpu.VMEM(self_weight.shape, BF16),
            pltpu.VMEM((targets, hidden), F32),
            pltpu.SemaphoreType.DMA((seed_blocks + 3,)),
            pltpu.SemaphoreType.DMA((2 * seed_blocks,)),
        ],
        compiler_params=params(),
        cost_estimate=pl.CostEstimate(
            flops=2 * targets * seeds.shape[1] * hidden, bytes_accessed=7 * 10**6, transcendentals=0
        ),
        name="stage",
    )(
        in_hbm(tile_block),
        in_hbm(live_count.reshape(1, -1)),
        in_hbm(tile_weight),
        in_hbm(table),
        in_hbm(seeds),
        in_hbm(self_weight),
        in_hbm(bias.reshape(1, -1)),
    )


def pick_rows(asked, table):
    owners, _, slots = asked.shape
    rows, width = table.shape
    pieces = 8
    return pl.pallas_call(
        pick_kernel,
        out_shape=pltpu.HBM((owners * slots, width), BF16),
        in_specs=[pl.BlockSpec(memory_space=pltpu.VMEM), pl.BlockSpec(memory_space=pltpu.VMEM)],
        out_specs=pl.BlockSpec(memory_space=pltpu.HBM),
        scratch_shapes=[
            pltpu.VMEM((owners * slots, rows), BF16),
            pltpu.VMEM((owners * slots, width), BF16),
            pltpu.SemaphoreType.DMA((pieces,)),
        ],
        compiler_params=params(),
        cost_estimate=pl.CostEstimate(
            flops=2 * owners * slots * rows * width, bytes_accessed=5 * 10**6, transcendentals=0
        ),
        name="pick_rows",
    )(asked, in_vmem(table))


def turned(left, right):
    return lax.dot_general(left, right, (((0,), (0,)), ((), ())), preferred_element_type=F32)


def units_of(grad, core, span):
    hidden = grad.shape[1]
    unit = lax.broadcasted_iota(jnp.int32, (hidden, hidden // 2), 0)
    place = lax.broadcasted_iota(jnp.int32, (hidden, hidden // 2), 1)
    chosen = unit == place + (place // span + core) * span
    return jnp.dot(grad, jnp.where(chosen, 1.0, 0.0).astype(BF16), preferred_element_type=F32).astype(BF16)


def layer_kernel(
    span, core_ref, adj_ref, rows_ref, neigh_ref, own_hbm, cot_hbm, send_ref, grad_ref, agg_ref,
    own_ref, cot_ref, sems,
):
    pairs = [(own_hbm, own_ref), (cot_hbm, cot_ref)]
    loads = [pltpu.make_async_copy(src, dst, sems.at[i]) for i, (src, dst) in enumerate(pairs)]
    for load in loads:
        load.start()
    agg_ref[...] = jnp.dot(adj_ref[...], rows_ref[...], preferred_element_type=F32).astype(BF16)
    for load in loads:
        load.wait()
    targets = grad_ref.shape[0]
    step = targets // 4
    for start in range(0, targets, step):
        part = slice(start, start + step)
        pre = own_ref[part, :] + jnp.dot(agg_ref[part, :], neigh_ref[...], preferred_element_type=F32)
        s = 1.0 / (1.0 + jnp.exp(-pre))
        slope = s * (1.0 + pre * (1.0 - s))
        grad_ref[part, :] = (cot_ref[part, :].astype(F32) * slope).astype(BF16)
    other = units_of(grad_ref[...], 1 - core_ref[0], span)
    send_ref[...] = turned(other, agg_ref[...]).astype(BF16)


def layer(core, adj, rows, neigh, own, cot, span):
    targets, fetched = adj.shape
    width, hidden = neigh.shape
    near, far = pl.BlockSpec(memory_space=pltpu.VMEM), pl.BlockSpec(memory_space=pltpu.HBM)
    return pl.pallas_call(
        functools.partial(layer_kernel, span),
        out_shape=(
            pltpu.VMEM((hidden // 2, width), BF16),
            pltpu.VMEM((targets, hidden), BF16),
            pltpu.VMEM((targets, width), BF16),
        ),
        in_specs=[pl.BlockSpec(memory_space=pltpu.SMEM), near, near, near, far, far],
        out_specs=(near, near, near),
        scratch_shapes=[
            pltpu.VMEM((targets, hidden), F32),
            pltpu.VMEM((targets, hidden), BF16),
            pltpu.SemaphoreType.DMA((2,)),
        ],
        compiler_params=params(),
        cost_estimate=pl.CostEstimate(
            flops=2 * targets * width * (fetched + 2 * hidden),
            bytes_accessed=8 * 10**6,
            transcendentals=targets * hidden,
        ),
        name="layer",
    )(core, adj, rows, neigh, in_hbm(own), in_hbm(cot))


def own_term_kernel(span, core_ref, grad_ref, agg_ref, keep_ref):
    keep_ref[...] = turned(units_of(grad_ref[...], core_ref[0], span), agg_ref[...])


def own_term(core, grad, agg, span):
    targets, hidden = grad.shape
    width = agg.shape[1]
    near = pl.BlockSpec(memory_space=pltpu.VMEM)
    return pl.pallas_call(
        functools.partial(own_term_kernel, span),
        out_shape=pltpu.VMEM((hidden // 2, width), F32),
        in_specs=[pl.BlockSpec(memory_space=pltpu.SMEM), near, near],
        out_specs=near,
        compiler_params=params(),
        cost_estimate=pl.CostEstimate(
            flops=2 * targets * (width + hidden) * (hidden // 2), bytes_accessed=2 * 10**6, transcendentals=0
        ),
        name="own_term",
    )(core, grad, agg)


def pair_kernel(core_ref, keep_ref, got_ref, pair_ref):
    blocks, span, width = pair_ref.shape
    cut = width // blocks
    total = (keep_ref[...] + got_ref[...].astype(F32)).astype(BF16)

    @pl.when(core_ref[0] == 0)
    def _():
        for x in range(blocks):
            pair_ref[x] = total[x * span : (x + 1) * span, :]

    @pl.when(core_ref[0] == 1)
    def _():
        for z in range(blocks):
            parts = [total[x * span : (x + 1) * span, z * cut : (z + 1) * cut] for x in range(blocks)]
            pair_ref[z] = jnp.concatenate(parts, axis=1)


def pair_sum(core, keep, got, blocks):
    rows, width = keep.shape
    near = pl.BlockSpec(memory_space=pltpu.VMEM)
    return pl.pallas_call(
        pair_kernel,
        out_shape=pltpu.VMEM((blocks, rows // blocks, width), BF16),
        in_specs=[pl.BlockSpec(memory_space=pltpu.SMEM), near, near],
        out_specs=near,
        compiler_params=params(),
        name="pair_sum",
    )(core, keep, got)


def by_core(sizes, first, second):
    ranks = np.arange(np.prod(sizes)).reshape(sizes)
    groups = []
    for core, axes in enumerate((first, second)):
        rest = [a for a in (0, 2, 3) if a not in axes]
        half = np.expand_dims(ranks[:, core], 1).transpose(*rest, 1, *axes)
        groups += half.reshape(-1, int(np.prod([sizes[a] for a in axes]))).tolist()
    return groups


def body(
    features,
    fetch_row,
    live_count,
    seed_features,
    tile_block,
    tile_weight,
    self_weight,
    neighbour_weight,
    layer_bias,
    cotangent,
):
    owners, slots = fetch_row.shape
    width, hidden = neighbour_weight.shape
    nx, nc, nz, ny = (lax.axis_size(a) for a in EVERY)
    span = hidden // (nx * nc)
    asked = lax.all_to_all(fetch_row.reshape(owners, 1, slots), GRP, split_axis=0, concat_axis=0, tiled=True)
    adj, own, table = stage(
        tile_block, live_count, tile_weight, features, seed_features, self_weight, layer_bias
    )
    picked = pick_rows(asked, table)
    rows = lax.all_to_all(picked.reshape(owners, slots, width), GRP, split_axis=0, concat_axis=0, tiled=True)
    core = lax.axis_index("c").astype(jnp.int32).reshape(1)
    send, grad, agg = layer(
        core, adj, rows.reshape(owners * slots, width), neighbour_weight, own, cotangent, span
    )
    got = lax.ppermute(send, "c", [(0, 1), (1, 0)])
    keep = own_term(core, grad, agg, span)
    sizes = (nx, nc, nz, ny)
    pair = pair_sum(core, keep, got, nx)
    parts = lax.all_to_all(
        pair, EVERY, split_axis=0, concat_axis=0, tiled=True, axis_index_groups=by_core(sizes, (0,), (2,))
    )
    ring = jnp.sum(parts.astype(F32), axis=0)
    cols = width // (nz * ny)
    pieces = ring.reshape(span, nz * ny, cols).transpose(1, 2, 0).reshape(nz * ny, cols * span)
    pieces = lax.all_to_all(
        pieces, EVERY, split_axis=0, concat_axis=0, tiled=True, axis_index_groups=by_core(sizes, (2, 3), (0, 3))
    )
    return jnp.sum(pieces, axis=0).reshape(cols, span).T


def solution(mesh):
    n_grp, n_rep = mesh.shape["grp"], mesh.shape["rep"]
    chips, lines = n_grp // 2, int(round(n_rep**0.5))
    fine = Mesh(mesh.devices.reshape(chips, 2, lines, n_rep // lines), EVERY)
    placed = (
        P(EVERY, None),
        P(GRP, REP),
        P(GRP, REP),
        P(EVERY, None),
        P(EVERY, None),
        P(EVERY, None, None, None),
        P(),
        P(),
        P(),
        P(EVERY, None),
    )
    return jax.shard_map(body, mesh=fine, in_specs=placed, out_specs=P(GRP, REP), check_vma=False)
```

```python
import functools

import jax
import jax.numpy as jnp
import numpy as np
from jax import lax
from jax.experimental import pallas as pl
from jax.experimental.pallas import tpu as pltpu
from jax.sharding import Mesh, PartitionSpec as P

F32 = jnp.float32
BF16 = jnp.bfloat16
GRP = ("x", "c")
REP = ("z", "y")
EVERY = GRP + REP
VMEM_LIMIT = 24 * 1024 * 1024


def in_vmem(array):
    return pltpu.with_memory_space_constraint(array, pltpu.VMEM)


def in_hbm(array):
    return pltpu.with_memory_space_constraint(array, pltpu.HBM)


def params():
    return pltpu.CompilerParams(vmem_limit_bytes=VMEM_LIMIT)


def pick_kernel(asked_ref, table_ref, out_ref, hot_ref, out_buf, out_sems):
    owners, slots = asked_ref.shape[0], asked_ref.shape[2]
    rows = table_ref.shape[0]
    line = lax.broadcasted_iota(jnp.int32, (slots, slots), 0)
    lane = lax.broadcasted_iota(jnp.int32, (slots, slots), 1)
    row_ix = lax.broadcasted_iota(jnp.int32, (slots, rows), 1).astype(F32)

    def build(first, last):
        for p in range(first, last):
            asked = jnp.broadcast_to(asked_ref[p].astype(F32), (slots, slots))
            column = jnp.sum(jnp.where(line == lane, asked, 0.0), axis=1, keepdims=True)
            hot_ref[p * slots : (p + 1) * slots, :] = jnp.where(row_ix == column, 1.0, 0.0).astype(BF16)

    pieces = out_sems.shape[0]
    each, early = owners // pieces, owners // 2
    size = each * slots
    build(0, early)
    stores = []
    for i in range(pieces):
        build(max(i * each, early), max((i + 1) * each, early))
        part = pl.ds(i * size, size)
        out_buf[part, :] = jnp.dot(hot_ref[part, :], table_ref[...], preferred_element_type=F32).astype(BF16)
        stores.append(pltpu.make_async_copy(out_buf.at[part], out_ref.at[part], out_sems.at[i]))
        stores[i].start()
    for store in stores:
        store.wait()


def stage_kernel(
    block_ref, live_ref, weight_hbm, table_hbm, seed_hbm, self_hbm, bias_ref, adj_hbm, own_hbm, table_ref,
    weight_ref, adj_ref, seed_ref, self_ref, own_ref, sems, out_sems,
):
    seed_blocks, tiles, side, _ = weight_ref.shape
    pairs = [(weight_hbm.at[b], weight_ref.at[b]) for b in range(seed_blocks)]
    pairs += [(seed_hbm, seed_ref), (self_hbm, self_ref), (table_hbm, table_ref)]
    loads = [pltpu.make_async_copy(src, dst, sems.at[i]) for i, (src, dst) in enumerate(pairs)]
    for load in loads:
        load.start()
    slots = adj_ref.shape[1] // live_ref.shape[1]
    lane = lax.broadcasted_iota(jnp.int32, (side, side), 1)
    stores = []
    for b in range(seed_blocks):
        loads[b].wait()
        lines = slice(b * side, (b + 1) * side)
        for k in range(tiles):
            block = block_ref[b, k]
            limit = jnp.where(lane < slots, live_ref[0, 2 * block], live_ref[0, 2 * block + 1] + slots)
            tile = jnp.where(lane < limit, weight_ref[b, k].astype(F32), 0.0)
            start = pl.multiple_of(block * side, side)
            adj_ref[lines, pl.ds(start, side)] = tile.astype(BF16)
        part = pl.ds(b * side, side)
        stores.append(pltpu.make_async_copy(adj_ref.at[part], adj_hbm.at[part], out_sems.at[b]))
        stores[b].start()
    for load in loads[seed_blocks:]:
        load.wait()
    for b in range(seed_blocks):
        part = pl.ds(b * side, side)
        own_ref[part, :] = jnp.dot(seed_ref[part, :], self_ref[...], preferred_element_type=F32) + bias_ref[...]
        stores.append(pltpu.make_async_copy(own_ref.at[part], own_hbm.at[part], out_sems.at[seed_blocks + b]))
        stores[seed_blocks + b].start()
    for store in stores:
        store.wait()


def stage(tile_block, live_count, tile_weight, table, seeds, self_weight, bias):
    seed_blocks, tiles, side, _ = tile_weight.shape
    targets, hidden = seeds.shape[0], self_weight.shape[1]
    near, far = pl.BlockSpec(memory_space=pltpu.VMEM), pl.BlockSpec(memory_space=pltpu.HBM)
    scalars = pl.BlockSpec(memory_space=pltpu.SMEM)
    shape = (seed_blocks * side, tiles * side)
    return pl.pallas_call(
        stage_kernel,
        out_shape=(pltpu.HBM(shape, BF16), pltpu.HBM((targets, hidden), F32), pltpu.VMEM(table.shape, BF16)),
        in_specs=[scalars, scalars, far, far, far, far, near],
        out_specs=(far, far, near),
        scratch_shapes=[
            pltpu.VMEM(tile_weight.shape, BF16),
            pltpu.VMEM(shape, BF16),
            pltpu.VMEM(seeds.shape, BF16),
            pltpu.VMEM(self_weight.shape, BF16),
            pltpu.VMEM((targets, hidden), F32),
            pltpu.SemaphoreType.DMA((seed_blocks + 3,)),
            pltpu.SemaphoreType.DMA((2 * seed_blocks,)),
        ],
        compiler_params=params(),
        cost_estimate=pl.CostEstimate(
            flops=2 * targets * seeds.shape[1] * hidden, bytes_accessed=7 * 10**6, transcendentals=0
        ),
        name="stage",
    )(
        in_hbm(tile_block),
        in_hbm(live_count.reshape(1, -1)),
        in_hbm(tile_weight),
        in_hbm(table),
        in_hbm(seeds),
        in_hbm(self_weight),
        in_hbm(bias.reshape(1, -1)),
    )


def pick_rows(asked, table):
    owners, _, slots = asked.shape
    rows, width = table.shape
    pieces = 8
    return pl.pallas_call(
        pick_kernel,
        out_shape=pltpu.HBM((owners * slots, width), BF16),
        in_specs=[pl.BlockSpec(memory_space=pltpu.VMEM), pl.BlockSpec(memory_space=pltpu.VMEM)],
        out_specs=pl.BlockSpec(memory_space=pltpu.HBM),
        scratch_shapes=[
            pltpu.VMEM((owners * slots, rows), BF16),
            pltpu.VMEM((owners * slots, width), BF16),
            pltpu.SemaphoreType.DMA((pieces,)),
        ],
        compiler_params=params(),
        cost_estimate=pl.CostEstimate(
            flops=2 * owners * slots * rows * width, bytes_accessed=5 * 10**6, transcendentals=0
        ),
        name="pick_rows",
    )(asked, in_vmem(table))


def turned(left, right):
    return lax.dot_general(left, right, (((0,), (0,)), ((), ())), preferred_element_type=F32)


def units_of(grad, core, span):
    hidden = grad.shape[1]
    unit = lax.broadcasted_iota(jnp.int32, (hidden, hidden // 2), 0)
    place = lax.broadcasted_iota(jnp.int32, (hidden, hidden // 2), 1)
    chosen = unit == place + (place // span + core) * span
    return jnp.dot(grad, jnp.where(chosen, 1.0, 0.0).astype(BF16), preferred_element_type=F32).astype(BF16)


def layer_kernel(
    span, core_ref, adj_ref, rows_ref, neigh_ref, own_hbm, cot_hbm, send_ref, grad_ref, agg_ref,
    own_ref, cot_ref, sems,
):
    pairs = [(own_hbm, own_ref), (cot_hbm, cot_ref)]
    loads = [pltpu.make_async_copy(src, dst, sems.at[i]) for i, (src, dst) in enumerate(pairs)]
    for load in loads:
        load.start()
    agg_ref[...] = jnp.dot(adj_ref[...], rows_ref[...], preferred_element_type=F32).astype(BF16)
    for load in loads:
        load.wait()
    targets = grad_ref.shape[0]
    step = targets // 4
    for start in range(0, targets, step):
        part = slice(start, start + step)
        pre = own_ref[part, :] + jnp.dot(agg_ref[part, :], neigh_ref[...], preferred_element_type=F32)
        s = 0.5 * jnp.tanh(0.5 * pre) + 0.5
        slope = s * (1.0 + pre * (1.0 - s))
        grad_ref[part, :] = (cot_ref[part, :].astype(F32) * slope).astype(BF16)
    other = units_of(grad_ref[...], 1 - core_ref[0], span)
    send_ref[...] = turned(other, agg_ref[...]).astype(BF16)


def layer(core, adj, rows, neigh, own, cot, span):
    targets, fetched = adj.shape
    width, hidden = neigh.shape
    near, far = pl.BlockSpec(memory_space=pltpu.VMEM), pl.BlockSpec(memory_space=pltpu.HBM)
    return pl.pallas_call(
        functools.partial(layer_kernel, span),
        out_shape=(
            pltpu.VMEM((hidden // 2, width), BF16),
            pltpu.VMEM((targets, hidden), BF16),
            pltpu.VMEM((targets, width), BF16),
        ),
        in_specs=[pl.BlockSpec(memory_space=pltpu.SMEM), near, near, near, far, far],
        out_specs=(near, near, near),
        scratch_shapes=[
            pltpu.VMEM((targets, hidden), F32),
            pltpu.VMEM((targets, hidden), BF16),
            pltpu.SemaphoreType.DMA((2,)),
        ],
        compiler_params=params(),
        cost_estimate=pl.CostEstimate(
            flops=2 * targets * width * (fetched + 2 * hidden),
            bytes_accessed=8 * 10**6,
            transcendentals=targets * hidden,
        ),
        name="layer",
    )(core, adj, rows, neigh, in_hbm(own), in_hbm(cot))


def own_term_kernel(span, core_ref, grad_ref, agg_ref, keep_ref):
    keep_ref[...] = turned(units_of(grad_ref[...], core_ref[0], span), agg_ref[...])


def own_term(core, grad, agg, span):
    targets, hidden = grad.shape
    width = agg.shape[1]
    near = pl.BlockSpec(memory_space=pltpu.VMEM)
    return pl.pallas_call(
        functools.partial(own_term_kernel, span),
        out_shape=pltpu.VMEM((hidden // 2, width), F32),
        in_specs=[pl.BlockSpec(memory_space=pltpu.SMEM), near, near],
        out_specs=near,
        compiler_params=params(),
        cost_estimate=pl.CostEstimate(
            flops=2 * targets * (width + hidden) * (hidden // 2), bytes_accessed=2 * 10**6, transcendentals=0
        ),
        name="own_term",
    )(core, grad, agg)


def pair_kernel(core_ref, keep_ref, got_ref, pair_ref):
    blocks, span, width = pair_ref.shape
    cut = width // blocks
    total = (keep_ref[...] + got_ref[...].astype(F32)).astype(BF16)

    @pl.when(core_ref[0] == 0)
    def _():
        for x in range(blocks):
            pair_ref[x] = total[x * span : (x + 1) * span, :]

    @pl.when(core_ref[0] == 1)
    def _():
        for z in range(blocks):
            parts = [total[x * span : (x + 1) * span, z * cut : (z + 1) * cut] for x in range(blocks)]
            pair_ref[z] = jnp.concatenate(parts, axis=1)


def pair_sum(core, keep, got, blocks):
    rows, width = keep.shape
    near = pl.BlockSpec(memory_space=pltpu.VMEM)
    return pl.pallas_call(
        pair_kernel,
        out_shape=pltpu.VMEM((blocks, rows // blocks, width), BF16),
        in_specs=[pl.BlockSpec(memory_space=pltpu.SMEM), near, near],
        out_specs=near,
        compiler_params=params(),
        name="pair_sum",
    )(core, keep, got)


def by_core(sizes, first, second):
    ranks = np.arange(np.prod(sizes)).reshape(sizes)
    groups = []
    for core, axes in enumerate((first, second)):
        rest = [a for a in (0, 2, 3) if a not in axes]
        half = np.expand_dims(ranks[:, core], 1).transpose(*rest, 1, *axes)
        groups += half.reshape(-1, int(np.prod([sizes[a] for a in axes]))).tolist()
    return groups


def body(
    features,
    fetch_row,
    live_count,
    seed_features,
    tile_block,
    tile_weight,
    self_weight,
    neighbour_weight,
    layer_bias,
    cotangent,
):
    owners, slots = fetch_row.shape
    width, hidden = neighbour_weight.shape
    nx, nc, nz, ny = (lax.axis_size(a) for a in EVERY)
    span = hidden // (nx * nc)
    asked = lax.all_to_all(fetch_row.reshape(owners, 1, slots), GRP, split_axis=0, concat_axis=0, tiled=True)
    adj, own, table = stage(
        tile_block, live_count, tile_weight, features, seed_features, self_weight, layer_bias
    )
    picked = pick_rows(asked, table)
    rows = lax.all_to_all(picked.reshape(owners, slots, width), GRP, split_axis=0, concat_axis=0, tiled=True)
    core = lax.axis_index("c").astype(jnp.int32).reshape(1)
    send, grad, agg = layer(
        core, adj, rows.reshape(owners * slots, width), neighbour_weight, own, cotangent, span
    )
    got = lax.ppermute(send, "c", [(0, 1), (1, 0)])
    keep = own_term(core, grad, agg, span)
    sizes = (nx, nc, nz, ny)
    pair = pair_sum(core, keep, got, nx)
    parts = lax.all_to_all(
        pair, EVERY, split_axis=0, concat_axis=0, tiled=True, axis_index_groups=by_core(sizes, (0,), (2,))
    )
    ring = jnp.sum(parts.astype(F32), axis=0)
    cols = width // (nz * ny)
    pieces = ring.reshape(span, nz * ny, cols).transpose(1, 2, 0).reshape(nz * ny, cols * span)
    pieces = lax.all_to_all(
        pieces, EVERY, split_axis=0, concat_axis=0, tiled=True, axis_index_groups=by_core(sizes, (2, 3), (0, 3))
    )
    return jnp.sum(pieces, axis=0).reshape(cols, span).T


def solution(mesh):
    n_grp, n_rep = mesh.shape["grp"], mesh.shape["rep"]
    chips, lines = n_grp // 2, int(round(n_rep**0.5))
    fine = Mesh(mesh.devices.reshape(chips, 2, lines, n_rep // lines), EVERY)
    placed = (
        P(EVERY, None),
        P(GRP, REP),
        P(GRP, REP),
        P(EVERY, None),
        P(EVERY, None),
        P(EVERY, None, None, None),
        P(),
        P(),
        P(),
        P(EVERY, None),
    )
    return jax.shard_map(body, mesh=fine, in_specs=placed, out_specs=P(GRP, REP), check_vma=False)
```
